128 devices in a mesh: section: 8 (over z, y_lo), ctx: 16 (over x, y_hi, core).
Axes of the slice: x: 4, y: 4 (y_hi: 2, y_lo: 2; y = y_hi * 2 + y_lo), z: 4, core: 2. Of those that a mesh axis runs over, the one named last changes fastest.
Arguments:
- queries: bfloat16 [16, 2560, 3072], P('section', 'ctx'), may hold values from -28 to 28, as said below
- cotangent: bfloat16 [16, 2560, 3072], P('section', 'ctx'), may hold values from -6 to 6
- ret_query: bfloat16 [2560, 3072], P('ctx', 'section'), may hold values from -6 to 6
- ret_key: bfloat16 [2560, 3072], P('ctx', 'section'), may hold values from -6 to 6
- ret_value: bfloat16 [2560, 3072], P('ctx', 'section'), may hold values from -6 to 6
- gate_log: float32 [2560, 24], P('ctx', 'section'), may hold values from -1.5 to 0, as said below
- kv_weight: bfloat16 [3072, 2048], P('section'), may hold values from -0.109375 to 0.109375
Outputs:
- attention: bfloat16 [16, 2560, 3072], P('section', 'ctx')
- query_grad: bfloat16 [16, 2560, 3072], P('section', 'ctx')
- retention_grad: bfloat16 [2560, 3072], P('ctx', 'section')
The draws below stay inside these ranges and needn't reach their ends.
Inputs may be any that keep to these rules, and one draw needn't show every extreme that they name: The attention queries are mostly of order one; a few rows may be scaled by up to 16. `gate_log`: every gate is below one.
All inputs are finite; a program needn't handle non-finite values.
Results may differ from the reference program's by a relative error of at most 0.034.
Values may be sent and summed in bfloat16 or wider, within the bound.
No kernel may reach another device: no remote copies, remote signals or barrier semaphores. Data moves between devices by JAX's collectives and lax.ppermute only.
A program may use at most 640 MiB of HBM per device.

```python
import math
import jax
import jax.numpy as jnp
from jax import lax

HEADS = 24
DH = 128
KV_HEADS = 8
D = 3072
N_LAYERS = 16
TOK_DEV = 160
TOKENS = 2560


def draw_queries(key, part):
    key = jax.random.fold_in(key, 11)
    first_key = jax.random.fold_in(key, 0)
    shape = (N_LAYERS, TOKENS, D)
    drawn = jnp.clip(jax.random.normal(first_key, shape, jnp.float32), -4.0, 4.0)
    return drawn.astype(jnp.bfloat16)


def draw_gate_log(key, part):
    key = jax.random.fold_in(key, 23)
    keys_list = jax.random.split(key, 6)
    fast_share = 0.5
    fast = jax.random.uniform(keys_list[0], (HEADS,), jnp.float32) < fast_share
    slow_rate = jnp.exp(jax.random.uniform(keys_list[1], (HEADS,), jnp.float32, math.log(0.1), math.log(0.9))) * (math.log(2.5) / TOKENS)
    fast_rate = jnp.exp(jax.random.uniform(keys_list[2], (HEADS,), jnp.float32, math.log(1.0 / 50.0), math.log(1.0 / 30.0)))
    per_channel_fading = jnp.where(fast, fast_rate, slow_rate)
    sampled_perturbation = jax.random.uniform(keys_list[3], (TOKENS, HEADS), jnp.float32, 0.5, 1.5)
    spots = jax.random.randint(keys_list[4], (2, HEADS), 0, TOKENS)
    objective_scores = jax.random.uniform(keys_list[5], (2, HEADS), jnp.float32, math.log(0.5), math.log(0.8))
    placed_sequence = jnp.arange(TOKENS, dtype=jnp.int32)[:, None, None] == spots[None]
    token_batches = jnp.sum(jnp.where(placed_sequence, objective_scores[None], 0.0), axis=1)
    return (token_batches - per_channel_fading[None, :] * sampled_perturbation).astype(jnp.float32)


def block_levels(stream_key, shape, cuts, least, high):
    def one(position, shards_of):
        steps = jax.random.uniform(jax.random.fold_in(jax.random.fold_in(stream_key, 6), position), (shards_of,), jnp.float32, least / len(cuts), high / len(cuts))
        return jnp.repeat(jnp.exp(steps), shape[position] // shards_of).reshape((-1,) + (1,) * (len(shape) - position - 1))

    factor_of = one(*cuts[0])
    for cut in cuts[1:]:
        factor_of = factor_of * one(*cut)
    return factor_of


def normal_values(key, extent, deviation, limit, pieces=(), kind=jnp.bfloat16):
    entries = deviation * jax.random.normal(key, extent, jnp.float32)
    if pieces:
        entries = entries * block_levels(key, extent, pieces, -0.22, 0.18)
    return jnp.clip(entries, -limit, limit).astype(kind)


def setup_inputs(seed: int = 0) -> dict:
    arg_keys = jax.random.split(jax.random.key(seed), 8)
    queries = draw_queries(jax.random.fold_in(arg_keys[7], 71), 0)
    cotangent = normal_values(arg_keys[1], (N_LAYERS, TOKENS, D), 1.0, 6.0, ((0, 8), (1, 16)))
    ret_query = normal_values(arg_keys[2], (TOKENS, D), 1.0, 6.0, ((0, 16), (1, 8)))
    ret_key = normal_values(arg_keys[3], (TOKENS, D), 1.0, 6.0, ((0, 16), (1, 8)))
    ret_value = normal_values(arg_keys[4], (TOKENS, D), 1.0, 6.0, ((0, 16), (1, 8)))
    gate_log = draw_gate_log(jax.random.fold_in(arg_keys[7], 71), 0)
    kv_weight = normal_values(arg_keys[6], (D, 2 * KV_HEADS * DH), D ** -0.5, 0.109375, ((0, 8),))
    return {"queries": queries, "cotangent": cotangent, "ret_query": ret_query, "ret_key": ret_key, "ret_value": ret_value, "gate_log": gate_log, "kv_weight": kv_weight}


epsilon = 1e-06
highest = lax.Precision.HIGHEST

def retention_block(state_before, inputs):
    query_part, key_part, value_part, gate_part = inputs
    cumulative = jnp.cumsum(gate_part, axis=0)
    places = jnp.arange(gate_part.shape[0], dtype=jnp.int32)
    causal = places[:, None] >= places[None, :]
    spread = cumulative.T[:, :, None] - cumulative.T[:, None, :]
    weights = jnp.exp(jnp.where(causal[None], spread, -jnp.inf))
    scores = jnp.einsum('thd,uhd->htu', query_part, key_part, precision=highest)
    inside = jnp.einsum('htu,uhd->thd', weights * scores, value_part, precision=highest)
    carried = jnp.einsum('thd,hde->the', query_part, state_before, precision=highest)
    raw_output = inside + jnp.exp(cumulative)[:, :, None] * carried
    tail_decay = jnp.exp(cumulative[-1][None, :] - cumulative)
    local_state = jnp.einsum('uh,uhd,uhe->hde', tail_decay, key_part, value_part, precision=highest)
    state_after = jnp.exp(cumulative[-1])[:, None, None] * state_before + local_state
    return (state_after, raw_output)

def reference(queries, cotangent, ret_query, ret_key, ret_value, gate_log, kv_weight):
    block_total = TOKENS // TOK_DEV

    def to_blocks(array):
        return array.astype(jnp.float32).reshape(block_total, TOK_DEV, HEADS, DH)
    gate_blocks = gate_log.reshape(block_total, TOK_DEV, HEADS)
    start_state = jnp.zeros((HEADS, DH, DH), jnp.float32)
    _, raw_output = lax.scan(retention_block, start_state, (to_blocks(ret_query), to_blocks(ret_key), to_blocks(ret_value), gate_blocks))
    raw_output = raw_output.reshape(TOKENS, HEADS, DH)
    normed = raw_output * lax.rsqrt(lax.optimization_barrier(jnp.mean(raw_output * raw_output, axis=-1, keepdims=True)) + epsilon)
    ret_out = normed.astype(jnp.bfloat16).reshape(TOKENS, D)
    cache = jnp.dot(ret_out, kv_weight, preferred_element_type=jnp.float32).astype(jnp.bfloat16)
    kv_width = KV_HEADS * DH
    cache_wide = lax.optimization_barrier(cache).astype(jnp.float32)
    cache_keys = cache_wide[:, :kv_width].reshape(TOKENS, KV_HEADS, DH)
    cache_values = cache_wide[:, kv_width:].reshape(TOKENS, KV_HEADS, DH)
    group_size = HEADS // KV_HEADS
    score_scale = 1.0 / math.sqrt(DH)
    block_rows = math.gcd(512, TOKENS)

    def one_layer(cache_term, layer_inputs):
        query_layer, grad_layer = layer_inputs
        attended_list = []
        grad_list = []
        for first_row in range(0, TOKENS, block_rows):
            last_row = first_row + block_rows
            query_block = query_layer[first_row:last_row].astype(jnp.float32).reshape(block_rows, KV_HEADS, group_size, DH)
            grad_block = grad_layer[first_row:last_row].astype(jnp.float32).reshape(block_rows, KV_HEADS, group_size, DH)
            key_block = cache_keys[:last_row]
            value_block = cache_values[:last_row]
            scores = jnp.einsum('rkgd,ukd->kgru', query_block, key_block, precision=highest) * score_scale
            visible = (first_row + jnp.arange(block_rows, dtype=jnp.int32))[:, None] >= jnp.arange(last_row, dtype=jnp.int32)[None, :]
            scores = jnp.where(visible, scores, -jnp.inf)
            row_top = lax.optimization_barrier(jnp.max(scores, axis=-1, keepdims=True))
            row_total = lax.optimization_barrier(jnp.sum(jnp.exp(scores - row_top), axis=-1, keepdims=True))
            soft_probs = jnp.exp(scores - row_top) / row_total
            probs_low = lax.optimization_barrier(soft_probs.astype(jnp.bfloat16)).astype(jnp.float32)
            mixed_output = jnp.einsum('kgru,ukd->rkgd', probs_low, value_block, precision=highest).astype(jnp.bfloat16)
            attended_wide = lax.optimization_barrier(mixed_output).astype(jnp.float32)
            row_delta = jnp.einsum('rkgd,rkgd->kgr', grad_block, attended_wide, precision=highest)
            prob_grad = jnp.einsum('rkgd,ukd->kgru', grad_block, value_block, precision=highest)
            score_grad = (soft_probs * (prob_grad - row_delta[..., None]) * score_scale).astype(jnp.bfloat16)
            score_wide = lax.optimization_barrier(score_grad).astype(jnp.float32)
            query_part = jnp.einsum('kgru,ukd->rkgd', score_wide, key_block, precision=highest).astype(jnp.bfloat16)
            key_grad = jnp.einsum('kgru,rkgd->ukd', score_wide, query_block, precision=highest)
            value_grad = jnp.einsum('kgru,rkgd->ukd', probs_low, grad_block, precision=highest)
            rows_term = jnp.concatenate([key_grad.reshape(last_row, kv_width), value_grad.reshape(last_row, kv_width)], axis=1)
            cache_term = cache_term.at[:last_row].add(rows_term)
            attended_list.append(mixed_output.reshape(block_rows, D))
            grad_list.append(query_part.reshape(block_rows, D))
        return (cache_term, (jnp.concatenate(attended_list, axis=0), jnp.concatenate(grad_list, axis=0)))
    start_term = jnp.zeros((TOKENS, 2 * kv_width), jnp.float32)
    cache_term, outputs = lax.scan(one_layer, start_term, (queries, cotangent))
    attention, query_grad = outputs
    cache_grad = cache_term.astype(jnp.bfloat16)
    retention_grad = jnp.dot(cache_grad, kv_weight.T, preferred_element_type=jnp.float32).astype(jnp.bfloat16)
    return (attention, query_grad, retention_grad)
```

```python
import functools
import math

import jax
import jax.numpy as jnp
from jax import lax
from jax.experimental import pallas as pl
from jax.experimental.pallas import tpu as pltpu
from jax.sharding import Mesh, PartitionSpec as P

F32 = jnp.float32
BF16 = jnp.bfloat16
DH = 128
TOK = 160
SECTION = ("z", "yl")
CTX = ("x", "yh", "core")
HEAD = ("x", "core")
BLOCK = ("z", "yl", "yh")
EVERY = SECTION + CTX
VMEM_LIMIT = 60 * 1024 * 1024
LOG2E = 1.4426950408889634
SCALE = 1.0 / math.sqrt(DH)
NT = (((1,), (1,)), ((), ()))
TN = (((0,), (0,)), ((), ()))


def transpose_pairs():
    pairs = []
    for s in range(8):
        for c in range(16):
            z, yl, yh = c // 4, (c // 2) % 2, c % 2
            x, core = s // 2, s % 2
            pairs.append((s * 16 + c, (z * 2 + yl) * 16 + x * 4 + yh * 2 + core))
    return pairs


TO_OWNER = transpose_pairs()
FROM_OWNER = [(b, a) for a, b in TO_OWNER]


def vmem(shape, dtype):
    return pltpu.VMEM(shape, dtype)


def whole():
    return pl.BlockSpec(memory_space=pltpu.VMEM)


def cumulate(gate):
    rows = gate.shape[0]
    lower = (
        lax.broadcasted_iota(jnp.int32, (rows, rows), 0)
        >= lax.broadcasted_iota(jnp.int32, (rows, rows), 1)
    ).astype(F32)
    return jnp.dot(lower, gate, precision=lax.Precision.HIGHEST, preferred_element_type=F32)


def split_rows(value):
    hi = value.astype(BF16)
    rest = value - hi.astype(F32)
    mid = rest.astype(BF16)
    low = (rest - mid.astype(F32)).astype(BF16)
    return hi, mid, low


def pack(packet_ref, states, logs):
    for h in range(3):
        packet_ref[h * DH : (h + 1) * DH, :] = states[h].astype(BF16)
    rows = []
    for h in range(3):
        rows.extend(split_rows(logs[h]))
    rows.append(jnp.zeros((7, DH), BF16))
    packet_ref[3 * DH :, :] = jnp.concatenate([r.astype(F32) for r in rows], axis=0).astype(BF16)


def unpack(packet_ref):
    states = [packet_ref[h * DH : (h + 1) * DH, :].astype(F32) for h in range(3)]
    tail = packet_ref[3 * DH :, :].astype(F32)
    logs = [tail[3 * h : 3 * h + 1] + tail[3 * h + 1 : 3 * h + 2] + tail[3 * h + 2 : 3 * h + 3] for h in range(3)]
    return states, logs


def local_state_kernel(k_ref, v_ref, gate_ref, packet_ref):
    cum = cumulate(gate_ref[...])
    last = cum[TOK - 1 : TOK, :]
    tail = jnp.exp(last - cum)
    states, logs = [], []
    for h in range(3):
        lanes = slice(h * DH, (h + 1) * DH)
        key = (k_ref[:, lanes].astype(F32) * tail[:, h : h + 1]).astype(BF16)
        states.append(lax.dot_general(key, v_ref[:, lanes], TN, preferred_element_type=F32))
        logs.append(jnp.broadcast_to(last[:, h : h + 1], (1, DH)))
    pack(packet_ref, states, logs)


def local_state(key, value, gate):
    return pl.pallas_call(
        local_state_kernel,
        out_shape=jax.ShapeDtypeStruct((3 * DH + 16, DH), BF16),
        in_specs=[whole()] * 3,
        out_specs=whole(),
    )(key, value, gate)


def group_kernel(place_ref, own_ref, a_ref, b_ref, c_ref, total_ref, prefix_ref):
    place = place_ref[0]
    parts = [unpack(r) for r in (own_ref, a_ref, b_ref, c_ref)]
    members = [place ^ k for k in range(4)]
    total_s, total_l, prefix_s, prefix_l = [], [], [], []
    for h in range(3):
        logs = [p[1][h] for p in parts]
        total = jnp.zeros((DH, DH), F32)
        prefix = jnp.zeros((DH, DH), F32)
        log_all = jnp.zeros((1, DH), F32)
        log_before = jnp.zeros((1, DH), F32)
        for j in range(4):
            after = jnp.zeros((1, DH), F32)
            between = jnp.zeros((1, DH), F32)
            for i in range(4):
                later = (members[i] > members[j]).astype(F32)
                after = after + logs[i] * later
                between = between + logs[i] * later * (members[i] < place).astype(F32)
            before = (members[j] < place).astype(F32)
            total = total + parts[j][0][h] * jnp.exp(after)
            prefix = prefix + parts[j][0][h] * (jnp.exp(between) * before)
            log_all = log_all + logs[j]
            log_before = log_before + logs[j] * before
        total_s.append(total)
        total_l.append(log_all)
        prefix_s.append(prefix)
        prefix_l.append(log_before)
    pack(total_ref, total_s, total_l)
    for h in range(3):
        prefix_ref[h] = prefix_s[h]
    prefix_ref[3] = jnp.concatenate(prefix_l + [jnp.zeros((DH - 3, DH), F32)], axis=0)


def group_totals(place, own, others):
    return pl.pallas_call(
        group_kernel,
        out_shape=[
            jax.ShapeDtypeStruct((3 * DH + 16, DH), BF16),
            jax.ShapeDtypeStruct((4, DH, DH), F32),
        ],
        in_specs=[pl.BlockSpec(memory_space=pltpu.SMEM)] + [whole()] * 4,
        out_specs=[whole()] * 2,
    )(place, own, *others)


def retention_kernel(place_ref, prefix_ref, a_ref, b_ref, c_ref, q_ref, k_ref, v_ref, gate_ref, w_ref, out_ref):
    place = place_ref[0]
    parts = [unpack(r) for r in (a_ref, b_ref, c_ref)]
    members = [lax.rem(place + 4 - k, 4) for k in range(1, 4)]
    cum = cumulate(gate_ref[...])
    cum_rows = jnp.concatenate([cum, jnp.zeros((TOK, DH - 3), F32)], axis=1).T
    causal = lax.broadcasted_iota(jnp.int32, (TOK, TOK), 0) >= lax.broadcasted_iota(
        jnp.int32, (TOK, TOK), 1
    )
    normed = []
    for h in range(3):
        lanes = slice(h * DH, (h + 1) * DH)
        logs = [p[1][h] for p in parts]
        before = jnp.zeros((DH, DH), F32)
        for j in range(3):
            between = jnp.zeros((1, DH), F32)
            for i in range(3):
                inside = jnp.logical_and(members[i] > members[j], members[i] < place).astype(F32)
                between = between + logs[i] * inside
            before = before + parts[j][0][h] * (jnp.exp(between) * (members[j] < place).astype(F32))
        state = before * jnp.exp(prefix_ref[3, h : h + 1, :]) + prefix_ref[h]
        column = cum[:, h : h + 1]
        spread = column - cum_rows[h : h + 1, :]
        weights = jnp.exp(jnp.where(causal, spread, -1e30))
        query = q_ref[:, lanes]
        scores = lax.dot_general(query, k_ref[:, lanes], NT, preferred_element_type=F32)
        raw = jnp.dot((weights * scores).astype(BF16), v_ref[:, lanes], preferred_element_type=F32)
        carried = jnp.dot(query, state.astype(BF16), preferred_element_type=F32)
        raw = raw + jnp.exp(column) * carried
        scale = lax.rsqrt(jnp.mean(raw * raw, axis=-1, keepdims=True) + 1e-6)
        normed.append((raw * scale).astype(BF16))
    rows = jnp.concatenate(normed, axis=1)
    for h in range(8):
        for part in range(2):
            lanes = slice(part * 8 * DH + h * DH, part * 8 * DH + (h + 1) * DH)
            out_ref[h, :, part * DH : (part + 1) * DH] = jnp.dot(
                rows, w_ref[:, lanes], preferred_element_type=F32
            ).astype(out_ref.dtype)


def retention(place, prefix, others, query, key, value, gate, weight):
    return pl.pallas_call(
        retention_kernel,
        out_shape=jax.ShapeDtypeStruct((8, TOK, 2 * DH), BF16),
        in_specs=[pl.BlockSpec(memory_space=pltpu.SMEM)] + [whole()] * 9,
        out_specs=whole(),
        compiler_params=pltpu.CompilerParams(vmem_limit_bytes=VMEM_LIMIT),
    )(place, prefix, *others, query, key, value, gate, weight)


CHUNK = 640
ROWS = 640
TK = 320


def attention_kernel(
    yh_ref, q_ref, do_ref, kv_ref, o_ref, dq_ref, dkv_ref, s_scr, p_scr, ds_scr, kt_scr, vt_scr, dk_acc, dv_acc
):
    step = pl.program_id(0)

    @pl.when(step == 0)
    def _():
        dk_acc[...] = jnp.zeros_like(dk_acc)
        dv_acc[...] = jnp.zeros_like(dv_acc)
        for b in range(4):
            rows = slice(b * CHUNK, (b + 1) * CHUNK)
            kt_scr[:, rows] = kv_ref[rows, :DH].astype(F32).T.astype(BF16)
            vt_scr[:, rows] = kv_ref[rows, DH:].astype(F32).T.astype(BF16)

    half = yh_ref[0] * 320
    lane = lax.broadcasted_iota(jnp.int32, (1, ROWS), 1)
    row_pos = half + TOK * (lane // 320) + lax.rem(lane, TOK)
    factor = SCALE * LOG2E
    for x in range(4):
        length = CHUNK * (x + 1)
        query = q_ref[2 * x : 2 * x + 2].reshape(ROWS, DH)
        grad = do_ref[2 * x : 2 * x + 2].reshape(ROWS, DH)

        def score_step(j, top):
            rows = pl.ds(pl.multiple_of(j * TK, TK), TK)
            s = lax.dot_general(kv_ref[rows, :DH], query, NT, preferred_element_type=F32)
            s_scr[rows, :] = s
            return jnp.maximum(top, jnp.max(s, axis=0, keepdims=True))

        def diag_step(j, top):
            rows = pl.ds(pl.multiple_of(x * CHUNK + j * TK, TK), TK)
            s = lax.dot_general(kv_ref[rows, :DH], query, NT, preferred_element_type=F32)
            key_pos = j * TK + lax.broadcasted_iota(jnp.int32, (TK, ROWS), 0)
            s = jnp.where(key_pos <= row_pos, s, -1e30)
            s_scr[rows, :] = s
            return jnp.maximum(top, jnp.max(s, axis=0, keepdims=True))

        top = jnp.full((1, ROWS), -1e30, F32)
        top = lax.fori_loop(0, x * CHUNK // TK, score_step, top)
        top = lax.fori_loop(0, CHUNK // TK, diag_step, top)
        top = top * factor

        def prob_step(j, total):
            rows = pl.ds(pl.multiple_of(j * TK, TK), TK)
            p = jnp.exp2(s_scr[rows, :] * factor - top)
            p_scr[rows, :] = p.astype(BF16)
            return total + jnp.sum(p, axis=0, keepdims=True)

        total = lax.fori_loop(0, length // TK, prob_step, jnp.zeros((1, ROWS), F32))
        inverse = 1.0 / total
        out_t = jnp.dot(vt_scr[:, :length], p_scr[:length, :], preferred_element_type=F32) * inverse
        out = out_t.T.astype(BF16)
        o_ref[2 * x : 2 * x + 2] = out.reshape(2, 2, TOK, DH)
        delta = jnp.sum((out.astype(F32) * grad.astype(F32)).T, axis=0, keepdims=True)
        inverse_col = jnp.broadcast_to(inverse, (DH, ROWS)).T
        grad_scaled = (grad.astype(F32) * inverse_col).astype(BF16)
        query_scaled = (query.astype(F32) * (inverse_col * SCALE)).astype(BF16)

        def grad_step(j, carry):
            rows = pl.ds(pl.multiple_of(j * TK, TK), TK)
            dp = lax.dot_general(kv_ref[rows, DH:], grad, NT, preferred_element_type=F32)
            p = p_scr[rows, :]
            ds = (p.astype(F32) * (dp - delta)).astype(BF16)
            ds_scr[rows, :] = ds
            dv_acc[rows, :] += jnp.dot(p, grad_scaled, preferred_element_type=F32)
            dk_acc[rows, :] += jnp.dot(ds, query_scaled, preferred_element_type=F32)
            return carry

        lax.fori_loop(0, length // TK, grad_step, 0)
        dq_t = jnp.dot(kt_scr[:, :length], ds_scr[:length, :], preferred_element_type=F32)
        dq = (dq_t * (inverse * SCALE)).T.astype(BF16)
        dq_ref[2 * x : 2 * x + 2] = dq.reshape(2, 2, TOK, DH)

    @pl.when(step == pl.num_programs(0) - 1)
    def _():
        dkv_ref[:, :DH] = dk_acc[...].astype(BF16)
        dkv_ref[:, DH:] = dv_acc[...].astype(BF16)


def attention_call(yh, queries, grads, cache):
    tokens = 4 * CHUNK
    by_head = pl.BlockSpec((8, 2, TOK, DH), lambda g: (0, 0, 0, g))
    const = pl.BlockSpec((tokens, 2 * DH), lambda g: (0, 0))
    return pl.pallas_call(
        attention_kernel,
        grid=(3,),
        out_shape=[
            jax.ShapeDtypeStruct((8, 2, TOK, 3 * DH), BF16),
            jax.ShapeDtypeStruct((8, 2, TOK, 3 * DH), BF16),
            jax.ShapeDtypeStruct((tokens, 2 * DH), BF16),
        ],
        in_specs=[pl.BlockSpec(memory_space=pltpu.SMEM), by_head, by_head, const],
        out_specs=[by_head, by_head, const],
        scratch_shapes=[
            vmem((tokens, ROWS), F32),
            vmem((tokens, ROWS), BF16),
            vmem((tokens, ROWS), BF16),
            vmem((DH, tokens), BF16),
            vmem((DH, tokens), BF16),
            vmem((tokens, DH), F32),
            vmem((tokens, DH), F32),
        ],
        compiler_params=pltpu.CompilerParams(vmem_limit_bytes=VMEM_LIMIT),
    )(yh, queries, grads, cache)


def project_kernel(g_ref, w_ref, out_ref):
    total = jnp.zeros(out_ref.shape, F32)
    for h in range(8):
        for part in range(2):
            lanes = slice(part * 8 * DH + h * DH, part * 8 * DH + (h + 1) * DH)
            total = total + lax.dot_general(
                g_ref[h, :, part * DH : (part + 1) * DH], w_ref[:, lanes], NT, preferred_element_type=F32
            )
    out_ref[...] = total.astype(BF16)


def project(grads, weight):
    return pl.pallas_call(
        project_kernel,
        out_shape=jax.ShapeDtypeStruct((TOK, weight.shape[0]), BF16),
        in_specs=[whole()] * 2,
        out_specs=whole(),
        compiler_params=pltpu.CompilerParams(vmem_limit_bytes=VMEM_LIMIT),
    )(grads, weight)


def exchange(value, axes):
    return lax.all_to_all(value, axes, 0, 0, tiled=True)


def gather_blocks(block, axes, count):
    return exchange(jnp.broadcast_to(block[None], (count,) + block.shape), axes)


def split_heads(rows):
    return rows.reshape(2, TOK, 8, 3 * DH).transpose(2, 0, 1, 3)


def join_heads(rows):
    return rows.transpose(1, 2, 0, 3).reshape(2, TOK, 24 * DH)


def body(queries, cotangent, ret_query, ret_key, ret_value, gate_log, kv_weight):
    x_place = lax.axis_index("x").astype(jnp.int32).reshape(1)
    yh_place = lax.axis_index("yh").astype(jnp.int32).reshape(1)
    in_group = (lax.axis_index("yh") * 2 + lax.axis_index("core")).astype(jnp.int32).reshape(1)
    q_heads = exchange(split_heads(queries), HEAD)
    do_heads = exchange(split_heads(cotangent), HEAD)

    packet = local_state(ret_key, ret_value, gate_log)
    near = [
        lax.ppermute(packet, ("yh", "core"), [(i, i ^ k) for i in range(4)]) for k in range(1, 4)
    ]
    total, prefix = group_totals(in_group, packet, near)
    far = [lax.ppermute(total, "x", [(i, (i + k) % 4) for i in range(4)]) for k in range(1, 4)]
    partial = retention(x_place, prefix, far, ret_query, ret_key, ret_value, gate_log, kv_weight)
    pieces = exchange(partial, SECTION)
    block = jnp.sum(pieces.astype(F32), axis=0).astype(BF16)
    block = lax.ppermute(block, EVERY, TO_OWNER)
    cache = gather_blocks(block, BLOCK, 16).reshape(16 * TOK, 2 * DH)

    attended, query_grad, cache_grad = attention_call(yh_place, q_heads, do_heads, cache)
    terms = exchange(cache_grad.reshape(16, TOK, 2 * DH), BLOCK)
    summed = jnp.sum(terms.astype(F32), axis=0).astype(BF16)
    summed = lax.ppermute(summed, EVERY, FROM_OWNER)
    grads = gather_blocks(summed, SECTION, 8)
    retention_grad = project(grads, kv_weight)
    attended = join_heads(exchange(attended, HEAD))
    query_grad = join_heads(exchange(query_grad, HEAD))
    return attended, query_grad, retention_grad


def solution(mesh):
    fine = Mesh(mesh.devices.reshape(4, 2, 4, 2, 2), EVERY)
    return jax.shard_map(
        body,
        mesh=fine,
        in_specs=(
            P(SECTION, CTX, None),
            P(SECTION, CTX, None),
            P(CTX, SECTION),
            P(CTX, SECTION),
            P(CTX, SECTION),
            P(CTX, SECTION),
            P(SECTION, None),
        ),
        out_specs=(P(SECTION, CTX, None), P(SECTION, CTX, None), P(CTX, SECTION)),
        check_vma=False,
    )
```

```python
import functools
import math

import jax
import jax.numpy as jnp
from jax import lax
from jax.experimental import pallas as pl
from jax.experimental.pallas import tpu as pltpu
from jax.sharding import Mesh, PartitionSpec as P

F32 = jnp.float32
BF16 = jnp.bfloat16
DH = 128
TOK = 160
TOKENS = 16 * TOK
SECTION = ("z", "yl")
CTX = ("x", "yh", "core")
HEAD = ("x", "core")
EVERY = SECTION + CTX
VMEM_LIMIT = 60 * 1024 * 1024
LOG2E = 1.4426950408889634
SCALE = 1.0 / math.sqrt(DH)
NT = (((1,), (1,)), ((), ()))
TN = (((0,), (0,)), ((), ()))


def owner_pairs(d):
    pairs = []
    for s in range(8):
        for c in range(16):
            h = 2 * (s // 2) + ((s % 2) ^ d)
            pairs.append((s * 16 + c, (c // 2) * 16 + (h // 2) * 4 + (c % 2) * 2 + h % 2))
    return pairs


TO_OWNER = [owner_pairs(d) for d in range(2)]
FROM_OWNER = [[(b, a) for a, b in pairs] for pairs in TO_OWNER]


def ring(k):
    return [(i, (i + k) % 4) for i in range(4)]


SWAP = [(0, 1), (1, 0)]


def vmem(shape, dtype):
    return pltpu.VMEM(shape, dtype)


def whole():
    return pl.BlockSpec(memory_space=pltpu.VMEM)


def cumulate(gate):
    rows = gate.shape[0]
    lower = (
        lax.broadcasted_iota(jnp.int32, (rows, rows), 0)
        >= lax.broadcasted_iota(jnp.int32, (rows, rows), 1)
    ).astype(F32)
    return jnp.dot(lower, gate, precision=lax.Precision.HIGHEST, preferred_element_type=F32)


def split_rows(value):
    hi = value.astype(BF16)
    rest = value - hi.astype(F32)
    mid = rest.astype(BF16)
    low = (rest - mid.astype(F32)).astype(BF16)
    return hi, mid, low


def pack(packet_ref, states, logs):
    for h in range(3):
        packet_ref[h * DH : (h + 1) * DH, :] = states[h].astype(BF16)
    rows = []
    for h in range(3):
        rows.extend(split_rows(logs[h]))
    rows.append(jnp.zeros((7, DH), BF16))
    packet_ref[3 * DH :, :] = jnp.concatenate([r.astype(F32) for r in rows], axis=0).astype(BF16)


def unpack(packet_ref):
    states = [packet_ref[h * DH : (h + 1) * DH, :].astype(F32) for h in range(3)]
    tail = packet_ref[3 * DH :, :].astype(F32)
    logs = [tail[3 * h : 3 * h + 1] + tail[3 * h + 1 : 3 * h + 2] + tail[3 * h + 2 : 3 * h + 3] for h in range(3)]
    return states, logs


def two_part(value):
    hi = value.astype(BF16)
    return hi, (value - hi.astype(F32)).astype(BF16)


def local_state_kernel(k_ref, v_ref, gate_ref, packet_ref):
    cum = cumulate(gate_ref[...])
    last = cum[TOK - 1 : TOK, :]
    tail = jnp.exp(last - cum)
    states, logs = [], []
    for h in range(3):
        lanes = slice(h * DH, (h + 1) * DH)
        hi, lo = two_part(k_ref[:, lanes].astype(F32) * tail[:, h : h + 1])
        value = v_ref[:, lanes]
        states.append(
            lax.dot_general(hi, value, TN, preferred_element_type=F32)
            + lax.dot_general(lo, value, TN, preferred_element_type=F32)
        )
        logs.append(jnp.broadcast_to(last[:, h : h + 1], (1, DH)))
    pack(packet_ref, states, logs)


def local_state(key, value, gate):
    return pl.pallas_call(
        local_state_kernel,
        out_shape=jax.ShapeDtypeStruct((3 * DH + 16, DH), BF16),
        in_specs=[whole()] * 3,
        out_specs=whole(),
    )(key, value, gate)


def group_kernel(place_ref, own_ref, a_ref, b_ref, c_ref, total_ref, prefix_ref):
    place = 2 * place_ref[4] + place_ref[2]
    parts = [unpack(r) for r in (own_ref, a_ref, b_ref, c_ref)]
    members = [place ^ k for k in range(4)]
    total_s, total_l, prefix_s, prefix_l = [], [], [], []
    for h in range(3):
        logs = [p[1][h] for p in parts]
        total = jnp.zeros((DH, DH), F32)
        prefix = jnp.zeros((DH, DH), F32)
        log_all = jnp.zeros((1, DH), F32)
        log_before = jnp.zeros((1, DH), F32)
        for j in range(4):
            after = jnp.zeros((1, DH), F32)
            between = jnp.zeros((1, DH), F32)
            for i in range(4):
                later = (members[i] > members[j]).astype(F32)
                after = after + logs[i] * later
                between = between + logs[i] * later * (members[i] < place).astype(F32)
            before = (members[j] < place).astype(F32)
            total = total + parts[j][0][h] * jnp.exp(after)
            prefix = prefix + parts[j][0][h] * (jnp.exp(between) * before)
            log_all = log_all + logs[j]
            log_before = log_before + logs[j] * before
        total_s.append(total)
        total_l.append(log_all)
        prefix_s.append(prefix)
        prefix_l.append(log_before)
    pack(total_ref, total_s, total_l)
    for h in range(3):
        prefix_ref[h] = prefix_s[h]
    prefix_ref[3] = jnp.concatenate(prefix_l + [jnp.zeros((DH - 3, DH), F32)], axis=0)


def group_totals(place, own, others):
    return pl.pallas_call(
        group_kernel,
        out_shape=[
            jax.ShapeDtypeStruct((3 * DH + 16, DH), BF16),
            jax.ShapeDtypeStruct((4, DH, DH), F32),
        ],
        in_specs=[pl.BlockSpec(memory_space=pltpu.SMEM)] + [whole()] * 4,
        out_specs=[whole()] * 2,
    )(place, own, *others)


def retention_kernel(place_ref, prefix_ref, a_ref, b_ref, c_ref, q_ref, k_ref, v_ref, gate_ref, w_ref, *out_refs):
    place = place_ref[3]
    parts = [unpack(r) for r in (a_ref, b_ref, c_ref)]
    members = [lax.rem(place + 4 - k, 4) for k in range(1, 4)]
    cum = cumulate(gate_ref[...])
    cum_rows = jnp.concatenate([cum, jnp.zeros((TOK, DH - 3), F32)], axis=1).T
    causal = lax.broadcasted_iota(jnp.int32, (TOK, TOK), 0) >= lax.broadcasted_iota(
        jnp.int32, (TOK, TOK), 1
    )
    normed = []
    for h in range(3):
        lanes = slice(h * DH, (h + 1) * DH)
        logs = [p[1][h] for p in parts]
        before = jnp.zeros((DH, DH), F32)
        for j in range(3):
            between = jnp.zeros((1, DH), F32)
            for i in range(3):
                inside = jnp.logical_and(members[i] > members[j], members[i] < place).astype(F32)
                between = between + logs[i] * inside
            before = before + parts[j][0][h] * (jnp.exp(between) * (members[j] < place).astype(F32))
        state = before * jnp.exp(prefix_ref[3, h : h + 1, :]) + prefix_ref[h]
        column = cum[:, h : h + 1]
        spread = column - cum_rows[h : h + 1, :]
        weights = jnp.exp(jnp.where(causal, spread, -1e30))
        query = q_ref[:, lanes]
        scores = lax.dot_general(query, k_ref[:, lanes], NT, preferred_element_type=F32)
        value = v_ref[:, lanes]
        hi, lo = two_part(weights * scores)
        raw = jnp.dot(hi, value, preferred_element_type=F32) + jnp.dot(lo, value, preferred_element_type=F32)
        hi, lo = two_part(state)
        carried = jnp.dot(query, hi, preferred_element_type=F32) + jnp.dot(query, lo, preferred_element_type=F32)
        raw = raw + jnp.exp(column) * carried
        scale = lax.rsqrt(jnp.mean(raw * raw, axis=-1, keepdims=True) + 1e-6)
        normed.append((raw * scale).astype(BF16))
    rows = jnp.concatenate(normed, axis=1)
    for k in range(4):
        for d in range(2):
            h = 2 * lax.rem(place_ref[0] + k, 4) + (place_ref[1] ^ d)
            for part in range(2):
                lanes = pl.ds(pl.multiple_of(part * 8 * DH + h * DH, DH), DH)
                out_refs[k][d, :, part * DH : (part + 1) * DH] = jnp.dot(
                    rows, w_ref[:, lanes], preferred_element_type=F32
                ).astype(BF16)


def retention(place, prefix, others, query, key, value, gate, weight):
    return pl.pallas_call(
        retention_kernel,
        out_shape=[jax.ShapeDtypeStruct((2, TOK, 2 * DH), BF16)] * 4,
        in_specs=[pl.BlockSpec(memory_space=pltpu.SMEM)] + [whole()] * 9,
        out_specs=[whole()] * 4,
        compiler_params=pltpu.CompilerParams(vmem_limit_bytes=VMEM_LIMIT),
    )(place, prefix, *others, query, key, value, gate, weight)


R = 256
SUB = 80
KT = 640
STAGES = (1, 2, 3, 4, 5)
UNITS = [(x, core, half) for x in range(4) for core in range(2) for half in range(2)]


class Unit:
    pass


def block_of(place_ref, k, e, d):
    z = lax.rem(place_ref[0] + k, 4)
    return 4 * z + 2 * (place_ref[1] ^ d) + (place_ref[4] ^ e)


def attention_kernel(first_call, last_call, place_ref, moved_ref, *refs):
    quads, refs = refs[:4], refs[4:]
    if not first_call:
        acc_ref, refs = refs[0], refs[1:]
    out_ref, refs = refs[0], refs[1:]
    grad_refs, scr = (refs[:4], refs[4:]) if last_call else (refs[:1], refs[1:])
    s_scr, p_scr, ds_scr = scr[0:2], scr[2:5], scr[5:7]
    out_acc, dq_acc, kt_scr, vt_scr, dk_acc, dv_acc, kv_scr = scr[7:]

    if first_call:
        dk_acc[...] = jnp.zeros_like(dk_acc)
        dv_acc[...] = jnp.zeros_like(dv_acc)
    else:
        dk_acc[...] = acc_ref[:, :DH]
        dv_acc[...] = acc_ref[:, DH:]
    for k in range(4):
        for e in range(2):
            for d in range(2):
                c = block_of(place_ref, 4 - k, e, d)
                kv_scr[pl.ds(pl.multiple_of(c * TOK, TOK), TOK), :] = quads[k][2 * e + d]
    for b in range(4):
        rows = slice(b * KT, (b + 1) * KT)
        kt_scr[:, rows] = kv_scr[rows, :DH].astype(F32).T.astype(BF16)
        vt_scr[:, rows] = kv_scr[rows, DH:].astype(F32).T.astype(BF16)

    factor = SCALE * LOG2E
    yh_rows = place_ref[4] * (2 * TOK)

    def fold(value, op):
        return op(value.reshape(value.shape[0] // 8, 8, R), axis=0)

    def read_rows(part, c):
        block = moved_ref[c.src, part, c.tokens, :]
        pieces = [block[:, g * DH : (g + 1) * DH] for g in range(3)]
        return jnp.concatenate(pieces + [jnp.zeros((R - 3 * SUB, DH), BF16)], axis=0)

    def write_rows(part, c, value):
        for g in range(3):
            out_ref[c.src, part, c.tokens, g * DH : (g + 1) * DH] = value[g * SUB : (g + 1) * SUB]

    def enter(n):
        c = Unit()
        c.x, core, half = UNITS[n]
        c.src, c.tokens = 2 * c.x + core, slice(half * SUB, (half + 1) * SUB)
        c.start = TOK * core + SUB * half
        c.last = -(-(2 * TOK + c.start + SUB) // DH) * DH
        c.s, c.p, c.ds = s_scr[n % 2], p_scr[n % 3], ds_scr[n % 2]
        c.q, c.g = read_rows(0, c), read_rows(1, c)
        c.qt = c.q.astype(F32).T.astype(BF16)
        c.gt = c.g.astype(F32).T.astype(BF16)
        c.top8 = jnp.full((8, R), -1e30, F32)
        c.sum8 = jnp.zeros((8, R), F32)
        return c

    def before(stage, c):
        if stage == 2:
            c.top = jnp.max(c.top8, axis=0, keepdims=True) * factor
        if stage == 3:
            c.inv = 1.0 / jnp.sum(c.sum8, axis=0, keepdims=True)
            col = jnp.broadcast_to(c.inv, (DH, R)).T
            c.gs = (c.g.astype(F32) * col).astype(BF16)
            c.qs = (c.q.astype(F32) * (col * SCALE)).astype(BF16)
        if stage == 4:
            out = (out_acc[...] * c.inv).T.astype(BF16)
            write_rows(0, c, out)
            c.delta = jnp.sum((out.astype(F32) * c.g.astype(F32)).T, axis=0, keepdims=True)

    def after(stage, c):
        if stage == 5:
            write_rows(1, c, (dq_acc[...] * (c.inv * SCALE)).T.astype(BF16))

    def work(stage, c, j, carry):
        diag = not isinstance(j, jax.Array) and j == c.x
        if isinstance(j, jax.Array):
            rows = pl.ds(pl.multiple_of(j * KT, KT), KT)
        else:
            rows = slice(j * KT, j * KT + (c.last if diag else KT))
        first = not isinstance(j, jax.Array) and j == 0
        if stage == 1:
            s = jnp.dot(kv_scr[rows, :DH], c.qt, preferred_element_type=F32)
            if diag:
                row = lax.rem(lax.broadcasted_iota(jnp.int32, (1, R), 1), SUB)
                visible = lax.broadcasted_iota(jnp.int32, (c.last, R), 0) <= row + (yh_rows + c.start)
                s = jnp.where(visible, s, -1e30)
            c.s[rows, :] = s
            return jnp.maximum(carry, fold(s, jnp.max))
        if stage == 2:
            p = jnp.exp2(c.s[rows, :] * factor - c.top)
            c.p[rows, :] = p.astype(BF16)
            return carry + fold(p, jnp.sum)
        if stage == 3:
            out = jnp.dot(vt_scr[:, rows], c.p[rows, :], preferred_element_type=F32)
            out_acc[...] = out if first else out_acc[...] + out
            dv_acc[rows, :] += jnp.dot(c.p[rows, :], c.gs, preferred_element_type=F32)
        if stage == 4:
            d = jnp.dot(kv_scr[rows, DH:], c.gt, preferred_element_type=F32)
            c.ds[rows, :] = (c.p[rows, :].astype(F32) * (d - c.delta)).astype(BF16)
        if stage == 5:
            dq = jnp.dot(kt_scr[:, rows], c.ds[rows, :], preferred_element_type=F32)
            dq_acc[...] = dq if first else dq_acc[...] + dq
            dk_acc[rows, :] += jnp.dot(c.ds[rows, :], c.qs, preferred_element_type=F32)
        return carry

    def get(stage, c):
        return c.top8 if stage == 1 else c.sum8 if stage == 2 else jnp.zeros((8, R), F32)

    def put(stage, c, value):
        if stage == 1:
            c.top8 = value
        if stage == 2:
            c.sum8 = value

    units = {}
    for n in range(len(UNITS) + 4):
        if n < len(UNITS):
            units[n] = enter(n)
        active = [(k, units[n - k + 1]) for k in STAGES if 0 <= n - k + 1 < len(UNITS)]
        for k, c in active:
            before(k, c)
        j = 0
        while j < 4:
            live = [(k, c) for k, c in active if j <= c.x]
            if not live:
                break
            carries = tuple(get(k, c) for k, c in live)
            if LOOPS and j == 1 and all(c.x == 3 for k, c in live):

                def step(t, carries, live=live):
                    return tuple(work(k, c, t, v) for (k, c), v in zip(live, carries))

                carries = lax.fori_loop(1, 3, step, carries)
                j = 3
            else:
                carries = tuple(work(k, c, j, v) for (k, c), v in zip(live, carries))
                j += 1
            for (k, c), v in zip(live, carries):
                put(k, c, v)
        for k, c in active:
            after(k, c)

    if not last_call:
        grad_refs[0][:, :DH] = dk_acc[...]
        grad_refs[0][:, DH:] = dv_acc[...]
        return
    for k in range(4):
        for e in range(2):
            for d in range(2):
                rows = pl.ds(pl.multiple_of(block_of(place_ref, k, e, d) * TOK, TOK), TOK)
                grad_refs[k][2 * e + d, :, :DH] = dk_acc[rows, :].astype(BF16)
                grad_refs[k][2 * e + d, :, DH:] = dv_acc[rows, :].astype(BF16)


LOOPS = True


def attention_call(place, moved, quads, acc, last):
    first = acc is None
    quad_shape = jax.ShapeDtypeStruct((4, TOK, 2 * DH), BF16)
    total_shape = jax.ShapeDtypeStruct((TOKENS, 2 * DH), F32)
    grads = [quad_shape] * 4 if last else [total_shape]
    return pl.pallas_call(
        functools.partial(attention_kernel, first, last),
        out_shape=[jax.ShapeDtypeStruct((8, 2, TOK, 3 * DH), BF16)] + grads,
        in_specs=[pl.BlockSpec(memory_space=pltpu.SMEM)] + [whole()] * (5 if first else 6),
        out_specs=[whole()] * (1 + len(grads)),
        scratch_shapes=[vmem((TOKENS, R), F32)] * 2
        + [vmem((TOKENS, R), BF16)] * 5
        + [vmem((DH, R), F32)] * 2
        + [vmem((DH, TOKENS), BF16)] * 2
        + [vmem((TOKENS, DH), F32)] * 2
        + [vmem((TOKENS, 2 * DH), BF16)],
        cost_estimate=pl.CostEstimate(
            flops=18 * TOKENS * TOKENS * DH, bytes_accessed=12 * TOKENS * DH * 2, transcendentals=TOKENS * TOKENS
        ),
        compiler_params=pltpu.CompilerParams(vmem_limit_bytes=VMEM_LIMIT),
    )(place, moved, *quads, *([] if first else [acc]))


def project_kernel(place_ref, *refs):
    pieces, w_ref, out_ref = refs[:4], refs[4], refs[5]
    total = jnp.zeros(out_ref.shape, F32)
    for k in range(4):
        for d in range(2):
            h = 2 * lax.rem(place_ref[0] + 4 - k, 4) + (place_ref[1] ^ d)
            for part in range(2):
                lanes = pl.ds(pl.multiple_of(part * 8 * DH + h * DH, DH), DH)
                total = total + lax.dot_general(
                    pieces[k][d, :, part * DH : (part + 1) * DH], w_ref[:, lanes], NT, preferred_element_type=F32
                )
    out_ref[...] = total.astype(BF16)


def project(place, pieces, weight):
    return pl.pallas_call(
        project_kernel,
        out_shape=jax.ShapeDtypeStruct((TOK, weight.shape[0]), BF16),
        in_specs=[pl.BlockSpec(memory_space=pltpu.SMEM)] + [whole()] * 5,
        out_specs=whole(),
        compiler_params=pltpu.CompilerParams(vmem_limit_bytes=VMEM_LIMIT),
    )(place, *pieces, weight)


def assemble_kernel(a_ref, b_ref, o_ref, dq_ref):
    layer = pl.program_id(0)
    for b, piece in enumerate((a_ref, b_ref)):

        @pl.when(layer == b)
        def _():
            for part, out_ref in enumerate((o_ref, dq_ref)):
                for h in range(8):
                    out_ref[0, :, 3 * h * DH : 3 * (h + 1) * DH] = piece[h, part]


def assemble(*pieces):
    return pl.pallas_call(
        assemble_kernel,
        grid=(2, 2),
        out_shape=[jax.ShapeDtypeStruct((2, TOK, 24 * DH), BF16)] * 2,
        in_specs=[
            pl.BlockSpec((8, 2, TOK // 2, 3 * DH), lambda b, t: (0, 0, jnp.where(b == 0, t, 1), 0)),
            pl.BlockSpec((8, 2, TOK // 2, 3 * DH), lambda b, t: (0, 0, jnp.where(b == 1, t, 0), 0)),
        ],
        out_specs=[pl.BlockSpec((1, TOK // 2, 24 * DH), lambda b, t: (b, t, 0))] * 2,
        compiler_params=pltpu.CompilerParams(vmem_limit_bytes=VMEM_LIMIT),
    )(*pieces)


def exchange(value, axes):
    return lax.all_to_all(value, axes, 0, 0, tiled=True)


def add(*terms):
    total = terms[0].astype(F32)
    for term in terms[1:]:
        total = total + term.astype(F32)
    return total.astype(BF16)


def by_head(queries, cotangent, layer):
    rows = jnp.stack([queries[layer], cotangent[layer]]).reshape(2, TOK, 8, 3 * DH)
    return rows.transpose(2, 0, 1, 3)


def body(queries, cotangent, ret_query, ret_key, ret_value, gate_log, kv_weight):
    place = jnp.stack([lax.axis_index(a) for a in ("z", "yl", "core", "x", "yh")]).astype(jnp.int32)
    inputs = [by_head(queries, cotangent, layer) for layer in range(2)]

    packet = local_state(ret_key, ret_value, gate_log)
    near = [
        lax.ppermute(packet, ("yh", "core"), [(i, i ^ k) for i in range(4)]) for k in range(1, 4)
    ]
    total, prefix = group_totals(place, packet, near)
    far = [lax.ppermute(total, "x", ring(k)) for k in range(1, 4)]
    parts = retention(place, prefix, far, ret_query, ret_key, ret_value, gate_log, kv_weight)

    heads = add(parts[0], *[lax.ppermute(parts[k], "z", ring(k)) for k in range(1, 4)])
    block = add(*[lax.ppermute(heads[d], EVERY, TO_OWNER[d]) for d in range(2)])
    inputs, block = lax.optimization_barrier((inputs, block))
    moved_a = exchange(inputs[0], HEAD)
    pair = jnp.stack([block, lax.ppermute(block, "yl", SWAP)])
    quad = jnp.concatenate([pair, lax.ppermute(pair, "yh", SWAP)], axis=0)
    quads = [quad] + [lax.ppermute(quad, "z", ring(k)) for k in range(1, 4)]
    quads, moved_a = lax.optimization_barrier((quads, moved_a))

    moved_b = exchange(inputs[1], HEAD)
    out_a, acc = attention_call(place, moved_a, quads, None, False)
    out_a, acc, moved_b = lax.optimization_barrier((out_a, acc, moved_b))
    back_a = exchange(out_a, HEAD)
    out_b, *grads = attention_call(place, moved_b, quads, acc, True)
    out_b, grads, back_a = lax.optimization_barrier((out_b, grads, back_a))
    back_b = exchange(out_b, HEAD)

    summed = add(grads[0], *[lax.ppermute(grads[k], "z", ring(k)) for k in range(1, 4)])
    summed = add(summed[:2], lax.ppermute(summed[2:], "yh", SWAP))
    summed = add(summed[0], lax.ppermute(summed[1], "yl", SWAP))
    pair = jnp.stack([lax.ppermute(summed, EVERY, FROM_OWNER[d]) for d in range(2)])
    grads = [pair] + [lax.ppermute(pair, "z", ring(k)) for k in range(1, 4)]
    attended, query_grad = assemble(back_a, back_b)
    grads, attended, query_grad = lax.optimization_barrier((grads, attended, query_grad))
    return attended, query_grad, project(place, grads, kv_weight)


def solution(mesh):
    fine = Mesh(mesh.devices.reshape(4, 2, 4, 2, 2), EVERY)
    return jax.shard_map(
        body,
        mesh=fine,
        in_specs=(
            P(SECTION, CTX, None),
            P(SECTION, CTX, None),
            P(CTX, SECTION),
            P(CTX, SECTION),
            P(CTX, SECTION),
            P(CTX, SECTION),
            P(SECTION, None),
        ),
        out_specs=(P(SECTION, CTX, None), P(SECTION, CTX, None), P(CTX, SECTION)),
        check_vma=False,
    )
```

```python
import functools
import math

import jax
import jax.numpy as jnp
from jax import lax
from jax.experimental import pallas as pl
from jax.experimental.pallas import tpu as pltpu
from jax.sharding import Mesh, PartitionSpec as P

F32 = jnp.float32
BF16 = jnp.bfloat16
DH = 128
TOK = 160
TOKENS = 16 * TOK
SECTION = ("z", "yl")
CTX = ("x", "yh", "core")
HEAD = ("x", "core")
EVERY = SECTION + CTX
VMEM_LIMIT = 60 * 1024 * 1024
LOG2E = 1.4426950408889634
SCALE = 1.0 / math.sqrt(DH)
NT = (((1,), (1,)), ((), ()))
TN = (((0,), (0,)), ((), ()))


def owner_pairs(d):
    pairs = []
    for z in range(4):
        for yl in range(2):
            for x in range(4):
                for yh in range(2):
                    for core in range(2):
                        here = (z * 2 + yl) * 16 + x * 4 + yh * 2 + core
                        there = (z * 2 + core) * 16 + ((x + z) % 4) * 4 + yh * 2 + (yl ^ d)
                        pairs.append((here, there))
    return pairs


TO_OWNER = [owner_pairs(d) for d in range(2)]
FROM_OWNER = [[(b, a) for a, b in pairs] for pairs in TO_OWNER]


def ring(k):
    return [(i, (i + k) % 4) for i in range(4)]


SWAP = [(0, 1), (1, 0)]


def vmem(shape, dtype):
    return pltpu.VMEM(shape, dtype)


def whole():
    return pl.BlockSpec(memory_space=pltpu.VMEM)


def cumulate(gate):
    rows = gate.shape[0]
    lower = (
        lax.broadcasted_iota(jnp.int32, (rows, rows), 0)
        >= lax.broadcasted_iota(jnp.int32, (rows, rows), 1)
    ).astype(F32)
    return jnp.dot(lower, gate, precision=lax.Precision.HIGHEST, preferred_element_type=F32)


def split_rows(value):
    hi = value.astype(BF16)
    rest = value - hi.astype(F32)
    mid = rest.astype(BF16)
    low = (rest - mid.astype(F32)).astype(BF16)
    return hi, mid, low


def pack(packet_ref, states, logs):
    for h in range(3):
        packet_ref[h * DH : (h + 1) * DH, :] = states[h].astype(BF16)
    rows = []
    for h in range(3):
        rows.extend(split_rows(logs[h]))
    rows.append(jnp.zeros((7, DH), BF16))
    packet_ref[3 * DH :, :] = jnp.concatenate([r.astype(F32) for r in rows], axis=0).astype(BF16)


def unpack(packet_ref):
    states = [packet_ref[h * DH : (h + 1) * DH, :].astype(F32) for h in range(3)]
    tail = packet_ref[3 * DH :, :].astype(F32)
    logs = [tail[3 * h : 3 * h + 1] + tail[3 * h + 1 : 3 * h + 2] + tail[3 * h + 2 : 3 * h + 3] for h in range(3)]
    return states, logs


def two_part(value):
    hi = value.astype(BF16)
    return hi, (value - hi.astype(F32)).astype(BF16)


def local_state_kernel(k_ref, v_ref, gate_ref, packet_ref):
    cum = cumulate(gate_ref[...])
    last = cum[TOK - 1 : TOK, :]
    tail = jnp.exp(last - cum)
    states, logs = [], []
    for h in range(3):
        lanes = slice(h * DH, (h + 1) * DH)
        hi, lo = two_part(k_ref[:, lanes].astype(F32) * tail[:, h : h + 1])
        value = v_ref[:, lanes]
        states.append(
            lax.dot_general(hi, value, TN, preferred_element_type=F32)
            + lax.dot_general(lo, value, TN, preferred_element_type=F32)
        )
        logs.append(jnp.broadcast_to(last[:, h : h + 1], (1, DH)))
    pack(packet_ref, states, logs)


def local_state(key, value, gate):
    return pl.pallas_call(
        local_state_kernel,
        out_shape=jax.ShapeDtypeStruct((3 * DH + 16, DH), BF16),
        in_specs=[whole()] * 3,
        out_specs=whole(),
    )(key, value, gate)


def group_kernel(place_ref, own_ref, a_ref, b_ref, c_ref, total_ref, prefix_ref):
    place = 2 * place_ref[4] + place_ref[2]
    parts = [unpack(r) for r in (own_ref, a_ref, b_ref, c_ref)]
    members = [place ^ k for k in range(4)]
    total_s, total_l, prefix_s, prefix_l = [], [], [], []
    for h in range(3):
        logs = [p[1][h] for p in parts]
        total = jnp.zeros((DH, DH), F32)
        prefix = jnp.zeros((DH, DH), F32)
        log_all = jnp.zeros((1, DH), F32)
        log_before = jnp.zeros((1, DH), F32)
        for j in range(4):
            after = jnp.zeros((1, DH), F32)
            between = jnp.zeros((1, DH), F32)
            for i in range(4):
                later = (members[i] > members[j]).astype(F32)
                after = after + logs[i] * later
                between = between + logs[i] * later * (members[i] < place).astype(F32)
            before = (members[j] < place).astype(F32)
            total = total + parts[j][0][h] * jnp.exp(after)
            prefix = prefix + parts[j][0][h] * (jnp.exp(between) * before)
            log_all = log_all + logs[j]
            log_before = log_before + logs[j] * before
        total_s.append(total)
        total_l.append(log_all)
        prefix_s.append(prefix)
        prefix_l.append(log_before)
    pack(total_ref, total_s, total_l)
    for h in range(3):
        prefix_ref[h] = prefix_s[h]
    prefix_ref[3] = jnp.concatenate(prefix_l + [jnp.zeros((DH - 3, DH), F32)], axis=0)


def group_totals(place, own, others):
    return pl.pallas_call(
        group_kernel,
        out_shape=[
            jax.ShapeDtypeStruct((3 * DH + 16, DH), BF16),
            jax.ShapeDtypeStruct((4, DH, DH), F32),
        ],
        in_specs=[pl.BlockSpec(memory_space=pltpu.SMEM)] + [whole()] * 4,
        out_specs=[whole()] * 2,
    )(place, own, *others)


def retention_kernel(place_ref, prefix_ref, a_ref, b_ref, c_ref, q_ref, k_ref, v_ref, gate_ref, w_ref, *out_refs):
    place = place_ref[3]
    parts = [unpack(r) for r in (a_ref, b_ref, c_ref)]
    members = [lax.rem(place + 4 - k, 4) for k in range(1, 4)]
    cum = cumulate(gate_ref[...])
    cum_rows = jnp.concatenate([cum, jnp.zeros((TOK, DH - 3), F32)], axis=1).T
    causal = lax.broadcasted_iota(jnp.int32, (TOK, TOK), 0) >= lax.broadcasted_iota(
        jnp.int32, (TOK, TOK), 1
    )
    normed = []
    for h in range(3):
        lanes = slice(h * DH, (h + 1) * DH)
        logs = [p[1][h] for p in parts]
        before = jnp.zeros((DH, DH), F32)
        for j in range(3):
            between = jnp.zeros((1, DH), F32)
            for i in range(3):
                inside = jnp.logical_and(members[i] > members[j], members[i] < place).astype(F32)
                between = between + logs[i] * inside
            before = before + parts[j][0][h] * (jnp.exp(between) * (members[j] < place).astype(F32))
        state = before * jnp.exp(prefix_ref[3, h : h + 1, :]) + prefix_ref[h]
        column = cum[:, h : h + 1]
        spread = column - cum_rows[h : h + 1, :]
        weights = jnp.exp(jnp.where(causal, spread, -1e30))
        query = q_ref[:, lanes]
        scores = lax.dot_general(query, k_ref[:, lanes], NT, preferred_element_type=F32)
        value = v_ref[:, lanes]
        hi, lo = two_part(weights * scores)
        raw = jnp.dot(hi, value, preferred_element_type=F32) + jnp.dot(lo, value, preferred_element_type=F32)
        hi, lo = two_part(state)
        carried = jnp.dot(query, hi, preferred_element_type=F32) + jnp.dot(query, lo, preferred_element_type=F32)
        raw = raw + jnp.exp(column) * carried
        scale = lax.rsqrt(jnp.mean(raw * raw, axis=-1, keepdims=True) + 1e-6)
        normed.append((raw * scale).astype(BF16))
    rows = jnp.concatenate(normed, axis=1)
    for k in range(4):
        for d in range(2):
            h = 2 * lax.rem(place_ref[0] + place_ref[3] + k, 4) + (place_ref[1] ^ d)
            for part in range(2):
                lanes = pl.ds(pl.multiple_of(part * 8 * DH + h * DH, DH), DH)
                out_refs[k][d, :, part * DH : (part + 1) * DH] = jnp.dot(
                    rows, w_ref[:, lanes], preferred_element_type=F32
                ).astype(BF16)


def retention(place, prefix, others, query, key, value, gate, weight):
    return pl.pallas_call(
        retention_kernel,
        out_shape=[jax.ShapeDtypeStruct((2, TOK, 2 * DH), BF16)] * 4,
        in_specs=[pl.BlockSpec(memory_space=pltpu.SMEM)] + [whole()] * 9,
        out_specs=[whole()] * 4,
        compiler_params=pltpu.CompilerParams(vmem_limit_bytes=VMEM_LIMIT),
    )(place, prefix, *others, query, key, value, gate, weight)


R = 256
SUB = 80
KT = 640
STAGES = (1, 2, 3, 4, 5)
UNITS = [(x, core, half) for x in range(4) for core in range(2) for half in range(2)]


class Unit:
    pass


def block_of(place_ref, k, e, d):
    x = lax.rem(place_ref[3] - place_ref[0] + 4 + k, 4)
    return 4 * x + 2 * (place_ref[4] ^ e) + (place_ref[1] ^ d)


def attention_kernel(first_call, last_call, place_ref, moved_ref, *refs):
    quads, refs = refs[:5], refs[5:]
    quads = [quads[0], quads[1], (quads[2], quads[3]), quads[4]]
    if not first_call:
        acc_ref, refs = refs[0], refs[1:]
    out_ref, refs = refs[0], refs[1:]
    grad_refs, scr = (refs[:4], refs[4:]) if last_call else (refs[:1], refs[1:])
    s_scr, p_scr, ds_scr = scr[0:2], scr[2:5], scr[5:7]
    out_acc, dq_acc, kt_scr, vt_scr, dk_acc, dv_acc, kv_scr = scr[7:]

    if first_call:
        dk_acc[...] = jnp.zeros_like(dk_acc)
        dv_acc[...] = jnp.zeros_like(dv_acc)
    else:
        dk_acc[...] = acc_ref[:, :DH]
        dv_acc[...] = acc_ref[:, DH:]
    for k in range(4):
        for e in range(2):
            for d in range(2):
                c = block_of(place_ref, k, e, d)
                piece = quads[k][e][d] if k == 2 else quads[k][2 * e + d]
                kv_scr[pl.ds(pl.multiple_of(c * TOK, TOK), TOK), :] = piece
    for b in range(4):
        rows = slice(b * KT, (b + 1) * KT)
        kt_scr[:, rows] = kv_scr[rows, :DH].astype(F32).T.astype(BF16)
        vt_scr[:, rows] = kv_scr[rows, DH:].astype(F32).T.astype(BF16)

    factor = SCALE * LOG2E
    yh_rows = place_ref[4] * (2 * TOK)

    def fold(value, op):
        return op(value.reshape(value.shape[0] // 8, 8, R), axis=0)

    def read_rows(part, c):
        block = moved_ref[c.src, part, c.tokens, :]
        pieces = [block[:, g * DH : (g + 1) * DH] for g in range(3)]
        return jnp.concatenate(pieces + [jnp.zeros((R - 3 * SUB, DH), BF16)], axis=0)

    def write_rows(part, c, value):
        for g in range(3):
            out_ref[c.src, part, c.tokens, g * DH : (g + 1) * DH] = value[g * SUB : (g + 1) * SUB]

    def enter(n):
        c = Unit()
        c.x, core, half = UNITS[n]
        c.src, c.tokens = 2 * c.x + core, slice(half * SUB, (half + 1) * SUB)
        c.start = TOK * core + SUB * half
        c.last = -(-(2 * TOK + c.start + SUB) // DH) * DH
        c.s, c.p, c.ds = s_scr[n % 2], p_scr[n % 3], ds_scr[n % 2]
        c.q, c.g = read_rows(0, c), read_rows(1, c)
        c.qt = c.q.astype(F32).T.astype(BF16)
        c.gt = c.g.astype(F32).T.astype(BF16)
        c.top8 = jnp.full((8, R), -1e30, F32)
        c.sum8 = jnp.zeros((8, R), F32)
        return c

    def before(stage, c):
        if stage == 2:
            c.top = jnp.max(c.top8, axis=0, keepdims=True) * factor
        if stage == 3:
            c.inv = 1.0 / jnp.sum(c.sum8, axis=0, keepdims=True)
            col = jnp.broadcast_to(c.inv, (DH, R)).T
            c.gs = (c.g.astype(F32) * col).astype(BF16)
            c.qs = (c.q.astype(F32) * (col * SCALE)).astype(BF16)
        if stage == 4:
            out = (out_acc[...] * c.inv).T.astype(BF16)
            write_rows(0, c, out)
            c.delta = jnp.sum((out.astype(F32) * c.g.astype(F32)).T, axis=0, keepdims=True)

    def after(stage, c):
        if stage == 5:
            write_rows(1, c, (dq_acc[...] * (c.inv * SCALE)).T.astype(BF16))

    def work(stage, c, j, carry):
        diag, first = j == c.x, j == 0
        rows = slice(j * KT, j * KT + (c.last if diag else KT))
        if stage == 1:
            s = jnp.dot(kv_scr[rows, :DH], c.qt, preferred_element_type=F32)
            if diag:
                row = lax.rem(lax.broadcasted_iota(jnp.int32, (1, R), 1), SUB)
                visible = lax.broadcasted_iota(jnp.int32, (c.last, R), 0) <= row + (yh_rows + c.start)
                s = jnp.where(visible, s, -1e30)
            c.s[rows, :] = s
            return jnp.maximum(carry, fold(s, jnp.max))
        if stage == 2:
            p = jnp.exp2(c.s[rows, :] * factor - c.top)
            c.p[rows, :] = p.astype(BF16)
            return carry + fold(p, jnp.sum)
        if stage == 3:
            out = jnp.dot(vt_scr[:, rows], c.p[rows, :], preferred_element_type=F32)
            out_acc[...] = out if first else out_acc[...] + out
            dv_acc[rows, :] += jnp.dot(c.p[rows, :], c.gs, preferred_element_type=F32)
        if stage == 4:
            d = jnp.dot(kv_scr[rows, DH:], c.gt, preferred_element_type=F32)
            c.ds[rows, :] = (c.p[rows, :].astype(F32) * (d - c.delta)).astype(BF16)
        if stage == 5:
            dq = jnp.dot(kt_scr[:, rows], c.ds[rows, :], preferred_element_type=F32)
            dq_acc[...] = dq if first else dq_acc[...] + dq
            dk_acc[rows, :] += jnp.dot(c.ds[rows, :], c.qs, preferred_element_type=F32)
        return carry

    def get(stage, c):
        return c.top8 if stage == 1 else c.sum8 if stage == 2 else jnp.zeros((8, R), F32)

    def put(stage, c, value):
        if stage == 1:
            c.top8 = value
        if stage == 2:
            c.sum8 = value

    units = {}
    for n in range(len(UNITS) + 4):
        if n < len(UNITS):
            units[n] = enter(n)
        active = [(k, units[n - k + 1]) for k in STAGES if 0 <= n - k + 1 < len(UNITS)]
        for k, c in active:
            before(k, c)
        j = 0
        while j < 4:
            live = [(k, c) for k, c in active if j <= c.x]
            if not live:
                break
            carries = tuple(get(k, c) for k, c in live)
            carries = tuple(work(k, c, j, v) for (k, c), v in zip(live, carries))
            j += 1
            for (k, c), v in zip(live, carries):
                put(k, c, v)
        for k, c in active:
            after(k, c)

    if not last_call:
        grad_refs[0][:, :DH] = dk_acc[...]
        grad_refs[0][:, DH:] = dv_acc[...]
        return
    for k in range(4):
        for e in range(2):
            for d in range(2):
                rows = pl.ds(pl.multiple_of(block_of(place_ref, 4 - k, e, d) * TOK, TOK), TOK)
                grad_refs[k][2 * e + d, :, :DH] = dk_acc[rows, :].astype(BF16)
                grad_refs[k][2 * e + d, :, DH:] = dv_acc[rows, :].astype(BF16)


def attention_call(place, moved, quads, acc, last):
    first = acc is None
    quad_shape = jax.ShapeDtypeStruct((4, TOK, 2 * DH), BF16)
    total_shape = jax.ShapeDtypeStruct((TOKENS, 2 * DH), F32)
    grads = [quad_shape] * 4 if last else [total_shape]
    return pl.pallas_call(
        functools.partial(attention_kernel, first, last),
        out_shape=[jax.ShapeDtypeStruct((8, 2, TOK, 3 * DH), BF16)] + grads,
        in_specs=[pl.BlockSpec(memory_space=pltpu.SMEM)] + [whole()] * (6 if first else 7),
        out_specs=[whole()] * (1 + len(grads)),
        scratch_shapes=[vmem((TOKENS, R), F32)] * 2
        + [vmem((TOKENS, R), BF16)] * 5
        + [vmem((DH, R), F32)] * 2
        + [vmem((DH, TOKENS), BF16)] * 2
        + [vmem((TOKENS, DH), F32)] * 2
        + [vmem((TOKENS, 2 * DH), BF16)],
        cost_estimate=pl.CostEstimate(
            flops=18 * TOKENS * TOKENS * DH, bytes_accessed=12 * TOKENS * DH * 2, transcendentals=TOKENS * TOKENS
        ),
        compiler_params=pltpu.CompilerParams(vmem_limit_bytes=VMEM_LIMIT),
    )(place, moved, *quads, *([] if first else [acc]))


def project_kernel(place_ref, *refs):
    pieces, w_ref, out_ref = refs[:4], refs[4], refs[5]
    total = jnp.zeros(out_ref.shape, F32)
    for k in range(4):
        for d in range(2):
            h = 2 * lax.rem(place_ref[0] + place_ref[3] + 4 - k, 4) + (place_ref[1] ^ d)
            for part in range(2):
                lanes = pl.ds(pl.multiple_of(part * 8 * DH + h * DH, DH), DH)
                total = total + lax.dot_general(
                    pieces[k][d, :, part * DH : (part + 1) * DH], w_ref[:, lanes], NT, preferred_element_type=F32
                )
    out_ref[...] = total.astype(BF16)


def project(place, pieces, weight):
    return pl.pallas_call(
        project_kernel,
        out_shape=jax.ShapeDtypeStruct((TOK, weight.shape[0]), BF16),
        in_specs=[pl.BlockSpec(memory_space=pltpu.SMEM)] + [whole()] * 5,
        out_specs=whole(),
        compiler_params=pltpu.CompilerParams(vmem_limit_bytes=VMEM_LIMIT),
    )(place, *pieces, weight)


def assemble_kernel(a_ref, b_ref, o_ref, dq_ref):
    layer = pl.program_id(0)
    for b, piece in enumerate((a_ref, b_ref)):

        @pl.when(layer == b)
        def _():
            for part, out_ref in enumerate((o_ref, dq_ref)):
                for h in range(8):
                    out_ref[0, :, 3 * h * DH : 3 * (h + 1) * DH] = piece[h, part]


def assemble(*pieces):
    return pl.pallas_call(
        assemble_kernel,
        grid=(2, 2),
        out_shape=[jax.ShapeDtypeStruct((2, TOK, 24 * DH), BF16)] * 2,
        in_specs=[
            pl.BlockSpec((8, 2, TOK // 2, 3 * DH), lambda b, t: (0, 0, jnp.where(b == 0, t, 1), 0)),
            pl.BlockSpec((8, 2, TOK // 2, 3 * DH), lambda b, t: (0, 0, jnp.where(b == 1, t, 0), 0)),
        ],
        out_specs=[pl.BlockSpec((1, TOK // 2, 24 * DH), lambda b, t: (b, t, 0))] * 2,
        compiler_params=pltpu.CompilerParams(vmem_limit_bytes=VMEM_LIMIT),
    )(*pieces)


def exchange(value, axes):
    return lax.all_to_all(value, axes, 0, 0, tiled=True)


def add(*terms):
    total = terms[0].astype(F32)
    for term in terms[1:]:
        total = total + term.astype(F32)
    return total.astype(BF16)


def by_head(queries, cotangent, layer):
    rows = jnp.stack([queries[layer], cotangent[layer]]).reshape(2, TOK, 8, 3 * DH)
    return rows.transpose(2, 0, 1, 3)


def body(queries, cotangent, ret_query, ret_key, ret_value, gate_log, kv_weight):
    place = jnp.stack([lax.axis_index(a) for a in ("z", "yl", "core", "x", "yh")]).astype(jnp.int32)
    inputs = [by_head(queries, cotangent, layer) for layer in range(2)]

    packet = local_state(ret_key, ret_value, gate_log)
    near = [
        lax.ppermute(packet, ("yh", "core"), [(i, i ^ k) for i in range(4)]) for k in range(1, 4)
    ]
    total, prefix = group_totals(place, packet, near)
    far = [lax.ppermute(total, "x", ring(k)) for k in range(1, 4)]
    inputs, far = lax.optimization_barrier((inputs, far))
    moved_a = exchange(inputs[0], HEAD)
    parts = retention(place, prefix, far, ret_query, ret_key, ret_value, gate_log, kv_weight)

    heads = add(parts[0], *[lax.ppermute(parts[k], "z", ring(k)) for k in range(1, 4)])
    block = add(*[lax.ppermute(heads[d], EVERY, TO_OWNER[d]) for d in range(2)])
    inputs, block, moved_a = lax.optimization_barrier((inputs, block, moved_a))
    moved_b = exchange(inputs[1], HEAD)
    pair = jnp.stack([block, lax.ppermute(block, "yl", SWAP)])
    quad = jnp.concatenate([pair, lax.ppermute(pair, "yh", SWAP)], axis=0)
    left, right = lax.ppermute(quad, "z", ring(1)), lax.ppermute(quad, "z", ring(3))
    across = lax.ppermute(left[:2], "z", ring(1)), lax.ppermute(right[2:], "z", ring(3))
    quads = [quad, left, *across, right]

    out_a, acc = attention_call(place, moved_a, quads, None, False)
    out_a, acc, moved_b = lax.optimization_barrier((out_a, acc, moved_b))
    back_a = exchange(out_a, HEAD)
    out_b, *grads = attention_call(place, moved_b, quads, acc, True)
    out_b, grads, back_a = lax.optimization_barrier((out_b, grads, back_a))
    back_b = exchange(out_b, HEAD)

    summed = add(grads[0], *[lax.ppermute(grads[k], "z", ring(k)) for k in range(1, 4)])
    summed = add(summed[:2], lax.ppermute(summed[2:], "yh", SWAP))
    summed = add(summed[0], lax.ppermute(summed[1], "yl", SWAP))
    pair = jnp.stack([lax.ppermute(summed, EVERY, FROM_OWNER[d]) for d in range(2)])
    grads = [pair] + [lax.ppermute(pair, "z", ring(k)) for k in range(1, 4)]
    attended, query_grad = assemble(back_a, back_b)
    grads, attended, query_grad = lax.optimization_barrier((grads, attended, query_grad))
    return attended, query_grad, project(place, grads, kv_weight)


def solution(mesh):
    fine = Mesh(mesh.devices.reshape(4, 2, 4, 2, 2), EVERY)
    return jax.shard_map(
        body,
        mesh=fine,
        in_specs=(
            P(SECTION, CTX, None),
            P(SECTION, CTX, None),
            P(CTX, SECTION),
            P(CTX, SECTION),
            P(CTX, SECTION),
            P(CTX, SECTION),
            P(SECTION, None),
        ),
        out_specs=(P(SECTION, CTX, None), P(SECTION, CTX, None), P(CTX, SECTION)),
        check_vma=False,
    )
```

```python
import functools
import math

import jax
import jax.numpy as jnp
from jax import lax
from jax.experimental import pallas as pl
from jax.experimental.pallas import tpu as pltpu
from jax.sharding import Mesh, PartitionSpec as P

F32 = jnp.float32
BF16 = jnp.bfloat16
DH = 128
TOK = 160
TOKENS = 16 * TOK
SECTION = ("z", "yl")
CTX = ("x", "yh", "core")
HEAD = ("x", "core")
EVERY = SECTION + CTX
VMEM_LIMIT = 60 * 1024 * 1024
LOG2E = 1.4426950408889634
SCALE = 1.0 / math.sqrt(DH)
NT = (((1,), (1,)), ((), ()))
TN = (((0,), (0,)), ((), ()))


def owner_pairs(d):
    pairs = []
    for z in range(4):
        for yl in range(2):
            for x in range(4):
                for yh in range(2):
                    for core in range(2):
                        here = (z * 2 + yl) * 16 + x * 4 + yh * 2 + core
                        there = (z * 2 + core) * 16 + ((x + z) % 4) * 4 + yh * 2 + (yl ^ d)
                        pairs.append((here, there))
    return pairs


TO_OWNER = [owner_pairs(d) for d in range(2)]
FROM_OWNER = [[(b, a) for a, b in pairs] for pairs in TO_OWNER]


def ring(k):
    return [(i, (i + k) % 4) for i in range(4)]


def flip(k):
    return [(i, i ^ k) for i in range(4)]


def vmem(shape, dtype):
    return pltpu.VMEM(shape, dtype)


def whole():
    return pl.BlockSpec(memory_space=pltpu.VMEM)


def cumulate(gate):
    rows = gate.shape[0]
    lower = (
        lax.broadcasted_iota(jnp.int32, (rows, rows), 0)
        >= lax.broadcasted_iota(jnp.int32, (rows, rows), 1)
    ).astype(F32)
    return jnp.dot(lower, gate, precision=lax.Precision.HIGHEST, preferred_element_type=F32)


def split_rows(value):
    hi = value.astype(BF16)
    rest = value - hi.astype(F32)
    mid = rest.astype(BF16)
    low = (rest - mid.astype(F32)).astype(BF16)
    return hi, mid, low


def pack(packet_ref, states, logs):
    for h in range(3):
        packet_ref[h * DH : (h + 1) * DH, :] = states[h].astype(BF16)
    rows = []
    for h in range(3):
        rows.extend(split_rows(logs[h]))
    rows.append(jnp.zeros((7, DH), BF16))
    packet_ref[3 * DH :, :] = jnp.concatenate([r.astype(F32) for r in rows], axis=0).astype(BF16)


def unpack(packet_ref):
    states = [packet_ref[h * DH : (h + 1) * DH, :].astype(F32) for h in range(3)]
    tail = packet_ref[3 * DH :, :].astype(F32)
    logs = [tail[3 * h : 3 * h + 1] + tail[3 * h + 1 : 3 * h + 2] + tail[3 * h + 2 : 3 * h + 3] for h in range(3)]
    return states, logs


def two_part(value):
    hi = value.astype(BF16)
    return hi, (value - hi.astype(F32)).astype(BF16)


def local_state_kernel(k_ref, v_ref, gate_ref, packet_ref):
    cum = cumulate(gate_ref[...])
    last = cum[TOK - 1 : TOK, :]
    tail = jnp.exp(last - cum)
    states, logs = [], []
    for h in range(3):
        lanes = slice(h * DH, (h + 1) * DH)
        hi, lo = two_part(k_ref[:, lanes].astype(F32) * tail[:, h : h + 1])
        value = v_ref[:, lanes]
        states.append(
            lax.dot_general(hi, value, TN, preferred_element_type=F32)
            + lax.dot_general(lo, value, TN, preferred_element_type=F32)
        )
        logs.append(jnp.broadcast_to(last[:, h : h + 1], (1, DH)))
    pack(packet_ref, states, logs)


def local_state(key, value, gate):
    return pl.pallas_call(
        local_state_kernel,
        out_shape=jax.ShapeDtypeStruct((3 * DH + 16, DH), BF16),
        in_specs=[whole()] * 3,
        out_specs=whole(),
    )(key, value, gate)


def group_kernel(place_ref, own_ref, a_ref, b_ref, c_ref, total_ref, prefix_ref):
    place = 2 * place_ref[4] + place_ref[2]
    parts = [unpack(r) for r in (own_ref, a_ref, b_ref, c_ref)]
    members = [place ^ k for k in range(4)]
    total_s, total_l, prefix_s, prefix_l = [], [], [], []
    for h in range(3):
        logs = [p[1][h] for p in parts]
        total = jnp.zeros((DH, DH), F32)
        prefix = jnp.zeros((DH, DH), F32)
        log_all = jnp.zeros((1, DH), F32)
        log_before = jnp.zeros((1, DH), F32)
        for j in range(4):
            after = jnp.zeros((1, DH), F32)
            between = jnp.zeros((1, DH), F32)
            for i in range(4):
                later = (members[i] > members[j]).astype(F32)
                after = after + logs[i] * later
                between = between + logs[i] * later * (members[i] < place).astype(F32)
            before = (members[j] < place).astype(F32)
            total = total + parts[j][0][h] * jnp.exp(after)
            prefix = prefix + parts[j][0][h] * (jnp.exp(between) * before)
            log_all = log_all + logs[j]
            log_before = log_before + logs[j] * before
        total_s.append(total)
        total_l.append(log_all)
        prefix_s.append(prefix)
        prefix_l.append(log_before)
    pack(total_ref, total_s, total_l)
    for h in range(3):
        prefix_ref[h] = prefix_s[h]
    prefix_ref[3] = jnp.concatenate(prefix_l + [jnp.zeros((DH - 3, DH), F32)], axis=0)


def group_totals(place, own, others):
    return pl.pallas_call(
        group_kernel,
        out_shape=[
            jax.ShapeDtypeStruct((3 * DH + 16, DH), BF16),
            jax.ShapeDtypeStruct((4, DH, DH), F32),
        ],
        in_specs=[pl.BlockSpec(memory_space=pltpu.SMEM)] + [whole()] * 4,
        out_specs=[whole()] * 2,
    )(place, own, *others)


def retention_kernel(place_ref, prefix_ref, a_ref, b_ref, c_ref, q_ref, k_ref, v_ref, gate_ref, w_ref, *out_refs):
    place = place_ref[3]
    parts = [unpack(r) for r in (a_ref, b_ref, c_ref)]
    members = [lax.rem(place + 4 - k, 4) for k in range(1, 4)]
    cum = cumulate(gate_ref[...])
    cum_rows = jnp.concatenate([cum, jnp.zeros((TOK, DH - 3), F32)], axis=1).T
    causal = lax.broadcasted_iota(jnp.int32, (TOK, TOK), 0) >= lax.broadcasted_iota(
        jnp.int32, (TOK, TOK), 1
    )
    normed = []
    for h in range(3):
        lanes = slice(h * DH, (h + 1) * DH)
        logs = [p[1][h] for p in parts]
        before = jnp.zeros((DH, DH), F32)
        for j in range(3):
            between = jnp.zeros((1, DH), F32)
            for i in range(3):
                inside = jnp.logical_and(members[i] > members[j], members[i] < place).astype(F32)
                between = between + logs[i] * inside
            before = before + parts[j][0][h] * (jnp.exp(between) * (members[j] < place).astype(F32))
        state = before * jnp.exp(prefix_ref[3, h : h + 1, :]) + prefix_ref[h]
        column = cum[:, h : h + 1]
        spread = column - cum_rows[h : h + 1, :]
        weights = jnp.exp(jnp.where(causal, spread, -1e30))
        query = q_ref[:, lanes]
        scores = lax.dot_general(query, k_ref[:, lanes], NT, preferred_element_type=F32)
        value = v_ref[:, lanes]
        hi, lo = two_part(weights * scores)
        raw = jnp.dot(hi, value, preferred_element_type=F32) + jnp.dot(lo, value, preferred_element_type=F32)
        hi, lo = two_part(state)
        carried = jnp.dot(query, hi, preferred_element_type=F32) + jnp.dot(query, lo, preferred_element_type=F32)
        raw = raw + jnp.exp(column) * carried
        scale = lax.rsqrt(jnp.mean(raw * raw, axis=-1, keepdims=True) + 1e-6)
        normed.append((raw * scale).astype(BF16))
    rows = jnp.concatenate(normed, axis=1)
    for k in range(4):
        for d in range(2):
            h = 2 * lax.rem(place_ref[0] + place_ref[3] + k, 4) + (place_ref[1] ^ d)
            for part in range(2):
                lanes = pl.ds(pl.multiple_of(part * 8 * DH + h * DH, DH), DH)
                out_refs[k][d, :, part * DH : (part + 1) * DH] = jnp.dot(
                    rows, w_ref[:, lanes], preferred_element_type=F32
                ).astype(BF16)


def retention(place, prefix, others, query, key, value, gate, weight):
    return pl.pallas_call(
        retention_kernel,
        out_shape=[jax.ShapeDtypeStruct((2, TOK, 2 * DH), BF16)] * 4,
        in_specs=[pl.BlockSpec(memory_space=pltpu.SMEM)] + [whole()] * 9,
        out_specs=[whole()] * 4,
        compiler_params=pltpu.CompilerParams(vmem_limit_bytes=VMEM_LIMIT),
    )(place, prefix, *others, query, key, value, gate, weight)


R = 256
SUB = 80
KT = 640
STAGES = (1, 2, 3, 4, 5)
UNITS = [(x, core, half) for x in (3, 2, 1, 0) for core in range(2) for half in range(2)]


class Unit:
    pass


def block_of(place_ref, k, e, d):
    x = lax.rem(place_ref[3] - place_ref[0] + 4 + k, 4)
    return 4 * x + 2 * (place_ref[4] ^ e) + (place_ref[1] ^ d)


def attention_kernel(first_call, last_call, place_ref, moved_ref, *refs):
    quads, refs = refs[:5], refs[5:]
    quads = [quads[0], quads[1], (quads[2], quads[3]), quads[4]]
    if not first_call:
        acc_ref, refs = refs[0], refs[1:]
    out_ref, refs = refs[0], refs[1:]
    grad_refs, scr = (refs[:4], refs[4:]) if last_call else (refs[:1], refs[1:])
    s_scr, p_scr, ds_scr = scr[0:2], scr[2:5], scr[5:7]
    out_acc, dq_acc, kt_scr, vt_scr, dk_acc, dv_acc, kv_scr = scr[7:]

    if first_call:
        dk_acc[...] = jnp.zeros_like(dk_acc)
        dv_acc[...] = jnp.zeros_like(dv_acc)
    else:
        dk_acc[...] = acc_ref[:, :DH]
        dv_acc[...] = acc_ref[:, DH:]
    for k in range(4):
        for e in range(2):
            for d in range(2):
                c = block_of(place_ref, k, e, d)
                piece = quads[k][e][d] if k == 2 else quads[k][2 * e + d]
                kv_scr[pl.ds(pl.multiple_of(c * TOK, TOK), TOK), :] = piece
    for b in range(4):
        rows = slice(b * KT, (b + 1) * KT)
        kt_scr[:, rows] = kv_scr[rows, :DH].astype(F32).T.astype(BF16)
        vt_scr[:, rows] = kv_scr[rows, DH:].astype(F32).T.astype(BF16)

    factor = SCALE * LOG2E
    yh_rows = place_ref[4] * (2 * TOK)

    def fold(value, op):
        return op(value.reshape(value.shape[0] // 8, 8, R), axis=0)

    def read_rows(part, c):
        block = moved_ref[c.src, part, c.tokens, :]
        pieces = [block[:, g * DH : (g + 1) * DH] for g in range(3)]
        return jnp.concatenate(pieces + [jnp.zeros((R - 3 * SUB, DH), BF16)], axis=0)

    def write_rows(part, c, value):
        for g in range(3):
            out_ref[c.src, part, c.tokens, g * DH : (g + 1) * DH] = value[g * SUB : (g + 1) * SUB]

    def enter(n):
        c = Unit()
        c.x, core, half = UNITS[n]
        c.src, c.tokens = 2 * c.x + core, slice(half * SUB, (half + 1) * SUB)
        c.start = TOK * core + SUB * half
        c.last = -(-(2 * TOK + c.start + SUB) // DH) * DH
        c.s, c.p, c.ds = s_scr[n % 2], p_scr[n % 3], ds_scr[n % 2]
        c.q, c.g = read_rows(0, c), read_rows(1, c)
        c.qt = c.q.astype(F32).T.astype(BF16)
        c.gt = c.g.astype(F32).T.astype(BF16)
        c.top8 = jnp.full((8, R), -1e30, F32)
        c.sum8 = jnp.zeros((8, R), F32)
        return c

    def before(stage, c):
        if stage == 2:
            c.top = jnp.max(c.top8, axis=0, keepdims=True) * factor
        if stage == 3:
            c.inv = 1.0 / jnp.sum(c.sum8, axis=0, keepdims=True)
            col = jnp.broadcast_to(c.inv, (DH, R)).T
            c.gs = (c.g.astype(F32) * col).astype(BF16)
            c.qs = (c.q.astype(F32) * (col * SCALE)).astype(BF16)
        if stage == 4:
            out = (out_acc[...] * c.inv).T.astype(BF16)
            write_rows(0, c, out)
            c.delta = jnp.sum((out.astype(F32) * c.g.astype(F32)).T, axis=0, keepdims=True)

    def after(stage, c):
        if stage == 5:
            write_rows(1, c, (dq_acc[...] * (c.inv * SCALE)).T.astype(BF16))

    def work(stage, c, j, carry):
        diag, first = j == c.x, j == 0
        rows = slice(j * KT, j * KT + (c.last if diag else KT))
        if stage == 1:
            s = jnp.dot(kv_scr[rows, :DH], c.qt, preferred_element_type=F32)
            if diag:
                row = lax.rem(lax.broadcasted_iota(jnp.int32, (1, R), 1), SUB)
                visible = lax.broadcasted_iota(jnp.int32, (c.last, R), 0) <= row + (yh_rows + c.start)
                s = jnp.where(visible, s, -1e30)
            c.s[rows, :] = s
            return jnp.maximum(carry, fold(s, jnp.max))
        if stage == 2:
            p = jnp.exp2(c.s[rows, :] * factor - c.top)
            c.p[rows, :] = p.astype(BF16)
            return carry + fold(p, jnp.sum)
        if stage == 3:
            out = jnp.dot(vt_scr[:, rows], c.p[rows, :], preferred_element_type=F32)
            out_acc[...] = out if first else out_acc[...] + out
            dv_acc[rows, :] += jnp.dot(c.p[rows, :], c.gs, preferred_element_type=F32)
        if stage == 4:
            d = jnp.dot(kv_scr[rows, DH:], c.gt, preferred_element_type=F32)
            c.ds[rows, :] = (c.p[rows, :].astype(F32) * (d - c.delta)).astype(BF16)
        if stage == 5:
            dq = jnp.dot(kt_scr[:, rows], c.ds[rows, :], preferred_element_type=F32)
            dq_acc[...] = dq if first else dq_acc[...] + dq
            dk_acc[rows, :] += jnp.dot(c.ds[rows, :], c.qs, preferred_element_type=F32)
        return carry

    def get(stage, c):
        return c.top8 if stage == 1 else c.sum8 if stage == 2 else jnp.zeros((8, R), F32)

    def put(stage, c, value):
        if stage == 1:
            c.top8 = value
        if stage == 2:
            c.sum8 = value

    units = {}
    for n in range(len(UNITS) + 4):
        if n < len(UNITS):
            units[n] = enter(n)
        active = [(k, units[n - k + 1]) for k in STAGES if 0 <= n - k + 1 < len(UNITS)]
        for k, c in active:
            before(k, c)
        j = 0
        while j < 4:
            live = [(k, c) for k, c in active if j <= c.x]
            if not live:
                break
            carries = tuple(get(k, c) for k, c in live)
            carries = tuple(work(k, c, j, v) for (k, c), v in zip(live, carries))
            j += 1
            for (k, c), v in zip(live, carries):
                put(k, c, v)
        for k, c in active:
            after(k, c)

    if not last_call:
        grad_refs[0][:, :DH] = dk_acc[...]
        grad_refs[0][:, DH:] = dv_acc[...]
        return
    for k in range(4):
        for e in range(2):
            for d in range(2):
                rows = pl.ds(pl.multiple_of(block_of(place_ref, 4 - k, e, d) * TOK, TOK), TOK)
                grad_refs[k][2 * e + d, :, :DH] = dk_acc[rows, :].astype(BF16)
                grad_refs[k][2 * e + d, :, DH:] = dv_acc[rows, :].astype(BF16)


def attention_call(place, moved, quads, acc, last):
    first = acc is None
    quad_shape = jax.ShapeDtypeStruct((4, TOK, 2 * DH), BF16)
    total_shape = jax.ShapeDtypeStruct((TOKENS, 2 * DH), F32)
    grads = [quad_shape] * 4 if last else [total_shape]
    return pl.pallas_call(
        functools.partial(attention_kernel, first, last),
        out_shape=[jax.ShapeDtypeStruct((8, 2, TOK, 3 * DH), BF16)] + grads,
        in_specs=[pl.BlockSpec(memory_space=pltpu.SMEM)] + [whole()] * (6 if first else 7),
        out_specs=[whole()] * (1 + len(grads)),
        scratch_shapes=[vmem((TOKENS, R), F32)] * 2
        + [vmem((TOKENS, R), BF16)] * 5
        + [vmem((DH, R), F32)] * 2
        + [vmem((DH, TOKENS), BF16)] * 2
        + [vmem((TOKENS, DH), F32)] * 2
        + [vmem((TOKENS, 2 * DH), BF16)],
        cost_estimate=pl.CostEstimate(
            flops=18 * TOKENS * TOKENS * DH, bytes_accessed=12 * TOKENS * DH * 2, transcendentals=TOKENS * TOKENS
        ),
        compiler_params=pltpu.CompilerParams(vmem_limit_bytes=VMEM_LIMIT),
    )(place, moved, *quads, *([] if first else [acc]))


def project_kernel(place_ref, *refs):
    pieces, w_ref, out_ref = refs[:4], refs[4], refs[5]
    total = jnp.zeros(out_ref.shape, F32)
    for k in range(4):
        for d in range(2):
            h = 2 * lax.rem(place_ref[0] + place_ref[3] + 4 - k, 4) + (place_ref[1] ^ d)
            for part in range(2):
                lanes = pl.ds(pl.multiple_of(part * 8 * DH + h * DH, DH), DH)
                total = total + lax.dot_general(
                    pieces[k][d, :, part * DH : (part + 1) * DH], w_ref[:, lanes], NT, preferred_element_type=F32
                )
    out_ref[...] = total.astype(BF16)


def project(place, pieces, weight):
    return pl.pallas_call(
        project_kernel,
        out_shape=jax.ShapeDtypeStruct((TOK, weight.shape[0]), BF16),
        in_specs=[pl.BlockSpec(memory_space=pltpu.SMEM)] + [whole()] * 5,
        out_specs=whole(),
        compiler_params=pltpu.CompilerParams(vmem_limit_bytes=VMEM_LIMIT),
    )(place, *pieces, weight)


def assemble_kernel(piece_ref, *refs):
    for part, out_ref in enumerate(refs[-2:]):
        for h in range(8):
            out_ref[0, :, 3 * h * DH : 3 * (h + 1) * DH] = piece_ref[h, part]


def assemble(layer, piece, filled):
    return pl.pallas_call(
        assemble_kernel,
        grid=(2,),
        out_shape=[jax.ShapeDtypeStruct((2, TOK, 24 * DH), BF16)] * 2,
        in_specs=[pl.BlockSpec((8, 2, TOK // 2, 3 * DH), lambda t: (0, 0, t, 0))]
        + [pl.BlockSpec(memory_space=pl.ANY)] * len(filled),
        out_specs=[pl.BlockSpec((1, TOK // 2, 24 * DH), lambda t: (layer, t, 0))] * 2,
        input_output_aliases={1: 0, 2: 1} if filled else {},
        compiler_params=pltpu.CompilerParams(vmem_limit_bytes=VMEM_LIMIT),
    )(piece, *filled)


def exchange(value, axes):
    return lax.all_to_all(value, axes, 0, 0, tiled=True)


def add(*terms):
    total = terms[0].astype(F32)
    for term in terms[1:]:
        total = total + term.astype(F32)
    return total.astype(BF16)


def by_head(queries, cotangent, layer):
    rows = jnp.stack([queries[layer], cotangent[layer]]).reshape(2, TOK, 8, 3 * DH)
    return rows.transpose(2, 0, 1, 3)


def body(queries, cotangent, ret_query, ret_key, ret_value, gate_log, kv_weight):
    place = jnp.stack([lax.axis_index(a) for a in ("z", "yl", "core", "x", "yh")]).astype(jnp.int32)
    inputs = [by_head(queries, cotangent, layer) for layer in range(2)]

    packet = local_state(ret_key, ret_value, gate_log)
    near = [
        lax.ppermute(packet, ("yh", "core"), flip(k)) for k in range(1, 4)
    ]
    total, prefix = group_totals(place, packet, near)
    far = [lax.ppermute(total, "x", ring(k)) for k in range(1, 4)]
    inputs, far = lax.optimization_barrier((inputs, far))
    moved_a = exchange(inputs[0], HEAD)
    parts = retention(place, prefix, far, ret_query, ret_key, ret_value, gate_log, kv_weight)

    heads = add(parts[0], *[lax.ppermute(parts[k], "z", ring(k)) for k in range(1, 4)])
    block = add(*[lax.ppermute(heads[d], EVERY, TO_OWNER[d]) for d in range(2)])
    inputs, block, moved_a = lax.optimization_barrier((inputs, block, moved_a))
    moved_b = exchange(inputs[1], HEAD)
    quad = jnp.stack([block] + [lax.ppermute(block, ("yl", "yh"), flip(k)) for k in (2, 1, 3)])
    left, right = lax.ppermute(quad, "z", ring(1)), lax.ppermute(quad, "z", ring(3))
    across = lax.ppermute(left[:2], "z", ring(1)), lax.ppermute(right[2:], "z", ring(3))
    quads = [quad, left, *across, right]

    out_a, acc = attention_call(place, moved_a, quads, None, False)
    out_a, acc, moved_b = lax.optimization_barrier((out_a, acc, moved_b))
    back_a = exchange(out_a, HEAD)
    out_b, *grads = attention_call(place, moved_b, quads, acc, True)
    out_b, grads, back_a = lax.optimization_barrier((out_b, grads, back_a))
    back_b = exchange(out_b, HEAD)

    summed = add(grads[0], *[lax.ppermute(grads[k], "z", ring(k)) for k in range(1, 4)])
    filled = assemble(0, back_a, ())
    summed, filled = lax.optimization_barrier((summed, filled))
    summed = add(summed[0], *[lax.ppermute(summed[i], ("yl", "yh"), flip(k)) for i, k in ((1, 2), (2, 1), (3, 3))])
    pair = jnp.stack([lax.ppermute(summed, EVERY, FROM_OWNER[d]) for d in range(2)])
    grads = [pair] + [lax.ppermute(pair, "z", ring(k)) for k in range(1, 4)]
    attended, query_grad = assemble(1, back_b, filled)
    grads, attended, query_grad = lax.optimization_barrier((grads, attended, query_grad))
    return attended, query_grad, project(place, grads, kv_weight)


def solution(mesh):
    fine = Mesh(mesh.devices.reshape(4, 2, 4, 2, 2), EVERY)
    return jax.shard_map(
        body,
        mesh=fine,
        in_specs=(
            P(SECTION, CTX, None),
            P(SECTION, CTX, None),
            P(CTX, SECTION),
            P(CTX, SECTION),
            P(CTX, SECTION),
            P(CTX, SECTION),
            P(SECTION, None),
        ),
        out_specs=(P(SECTION, CTX, None), P(SECTION, CTX, None), P(CTX, SECTION)),
        check_vma=False,
    )
```
